32 devices in a mesh: row: 4 (over y, core), col: 8 (over z, x).
Axes of the slice: x: 2, y: 2, z: 4, core: 2. Of those that a mesh axis runs over, the one named last changes fastest.
Arguments:
- points: bfloat16 [262144, 768], P(('row', 'col')), may hold values from -6 to 6
- node_of_row: int32 [262144], P(('row', 'col')), may hold values from 0 to 63, as said below
- init_axes: float32 [768, 8], replicated, may hold values from -0.21875 to 0.21875
Outputs:
- projected: float32 [8, 262144], P(None, ('row', 'col'))
The draws below stay inside these ranges and needn't reach their ends.
Inputs may be any that keep to these rules, and one draw needn't show every extreme that they name: `node_of_row`: never falls along the points; every one of the 64 nodes has at least 512 points; the points of one device belong to at most 8 nodes, and exactly 8 on some device; a node may cover many devices.
All inputs are finite; a program needn't handle non-finite values.
Results may differ from the reference program's by a relative error of at most 0.0035.
The reference program's roundings to bfloat16 on the way (of `lifted`) count: a program that leaves them out, or rounds other values in their place, can miss the bound.
Values sent between devices are 32-bit elements; how exact they have to be, the bound alone decides.
No kernel may reach another device: no remote copies, remote signals or barrier semaphores. Data moves between devices by JAX's collectives and lax.ppermute only.
A program may use at most 128 MiB of HBM per device.

```python
import jax
import jax.numpy as jnp
from jax import lax

D = 768
AXES = 8
ITERS = 3
SPAN_MOST = 8
TOK_DEV = 8192
NODES = 64
TOTAL = 262144
GAP = 512
DEVICES = 32


def draw_node_of_row(key, part):
    key_device = jax.random.fold_in(key, 11)
    key_choose = jax.random.fold_in(key, 12)
    key_places = jax.random.fold_in(key, 13)
    key_run = jax.random.fold_in(key, 14)
    cut_slots = SPAN_MOST - 1
    slot_total = DEVICES * cut_slots
    run_length = DEVICES // 2 + 1
    run_start = jax.random.randint(key_run, (), 0, DEVICES - run_length + 1)
    pick = jax.random.randint(key_device, (), 0, DEVICES - run_length)
    favoured = jnp.where(pick < run_start, pick, pick + run_length)
    slot_index = jnp.arange(slot_total, dtype=jnp.int32)
    slot_device = slot_index // cut_slots
    scores = jax.random.permutation(key_choose, slot_total).astype(jnp.int32)
    in_run = (slot_device >= run_start) & (slot_device < run_start + run_length)
    scores = jnp.where(in_run, slot_total + 1, scores)
    scores = jnp.where(slot_device == favoured, -1 - slot_index % cut_slots, scores)
    ranked = jnp.argsort(scores, stable=True)
    chosen = jnp.zeros((slot_total,), jnp.int32).at[ranked[:NODES - 1]].set(1)
    device_keys = jax.random.split(key_places, DEVICES)
    free_range = TOK_DEV - SPAN_MOST * GAP + cut_slots
    stride = jnp.arange(cut_slots, dtype=jnp.int32) * (GAP - 1) + GAP

    def place_cuts(one_key):
        picked = jnp.sort(jax.random.permutation(one_key, free_range)[:cut_slots].astype(jnp.int32))
        return picked + stride
    places = jax.vmap(place_cuts)(device_keys)
    positions = (jnp.arange(DEVICES, dtype=jnp.int32)[:, None] * TOK_DEV + places.astype(jnp.int32)).reshape(-1)
    cuts = jnp.zeros((TOTAL,), jnp.int32).at[positions].add(chosen)
    return jnp.cumsum(cuts).astype(jnp.int32)


def block_levels(own_key, dims, cuts, least, largest):
    factor_of, own = 1.0, jax.random.fold_in(own_key, 6)
    for position, blocks in cuts:
        heights = jnp.exp(jax.random.uniform(jax.random.fold_in(own, position), (blocks,), jnp.float32, least / len(cuts), largest / len(cuts)))
        factor_of = factor_of * jnp.repeat(heights, dims[position] // blocks).reshape([-1 if axis == position else 1 for axis in range(len(dims))])
    return factor_of


def centred(stream_key, dims, scale, reach, pieces=(), kind=jnp.bfloat16):
    array = jax.random.normal(stream_key, dims, jnp.float32) * scale
    if len(pieces) > 0:
        array = block_levels(stream_key, dims, pieces, -0.22, 0.18) * array
    return jnp.clip(array, min=-reach, max=reach).astype(kind)


def setup_inputs(seed: int = 0) -> dict:
    streams_of = jax.random.split(jax.random.key(seed), 4)
    return {
        "points": centred(streams_of[0], (TOTAL, D), 1.0, 6.0, ((0, 32),)),
        "node_of_row": draw_node_of_row(jax.random.fold_in(streams_of[3], 71), 0),
        "init_axes": centred(streams_of[2], (D, AXES), D ** -0.5, 0.21875, (), jnp.float32),
    }


def orthonormal(moment):
    found = []
    for index in range(moment.shape[1]):
        vector = moment[:, index]
        for column in found:
            vector = vector - jnp.sum(column * vector) * column
        vector = vector / jnp.sqrt(jnp.sum(vector * vector))
        found.append(vector)
    return jnp.stack(found, 1)

def window_member(node_ids):
    first_node = node_ids[0]
    member = node_ids[:, None] - first_node == jnp.arange(SPAN_MOST, dtype=jnp.int32)[None, :]
    return (first_node, member.astype(jnp.float32))

def lifted_terms(block, frames, centre):
    offset = jnp.einsum('ld,ldk->lk', centre, frames, precision=lax.Precision.HIGHEST)
    flat_frames = frames.astype(jnp.bfloat16).transpose(1, 0, 2).reshape(frames.shape[1], -1)
    spread = jnp.dot(block, flat_frames, preferred_element_type=jnp.float32)
    return spread.reshape(block.shape[0], SPAN_MOST, AXES) - offset[None]

def local_moment(block, member, frames, centre):
    terms = lifted_terms(block, frames, centre)
    lifted = terms.astype(jnp.bfloat16) * member.astype(jnp.bfloat16)[:, :, None]
    moment = lax.dot_general(block, lifted.reshape(block.shape[0], -1), (((0,), (0,)), ((), ())), preferred_element_type=jnp.float32)
    moment = moment.reshape(block.shape[1], SPAN_MOST, AXES).transpose(1, 0, 2)
    column_sums = lax.optimization_barrier(jnp.sum(lifted.astype(jnp.float32), 0))
    return moment - centre[:, :, None] * column_sums[:, None, :]

def add_window(total, first_node, piece):
    current = lax.dynamic_slice_in_dim(total, first_node, SPAN_MOST, 0)
    return lax.dynamic_update_slice_in_dim(total, current + piece, first_node, 0)

def reference(points, node_of_row, init_axes):
    width = points.shape[1]
    blocks = points.reshape(DEVICES, TOK_DEV, width)
    id_blocks = node_of_row.reshape(DEVICES, TOK_DEV)
    padded = NODES + SPAN_MOST

    def mean_block(carry, item):
        node_sums, node_counts = carry
        block, node_ids = item
        first_node, member = window_member(node_ids)
        sums = lax.dot_general(member.astype(jnp.bfloat16), block, (((0,), (0,)), ((), ())), preferred_element_type=jnp.float32)
        counts = lax.optimization_barrier(jnp.sum(member, 0))
        return ((add_window(node_sums, first_node, sums), add_window(node_counts, first_node, counts)), None)
    start = (jnp.zeros((padded, width), jnp.float32), jnp.zeros((padded,), jnp.float32))
    (node_sums, node_counts), _ = lax.scan(mean_block, start, (blocks, id_blocks))
    centre = node_sums[:NODES] / node_counts[:NODES, None]
    centre_pad = jnp.concatenate([centre, jnp.zeros((SPAN_MOST, width), jnp.float32)], 0)
    frames_pad = jnp.broadcast_to(init_axes.astype(jnp.float32), (padded, width, AXES))
    for repeat in range(ITERS):

        def sweep_block(carry, item):
            block, node_ids = item
            first_node, member = window_member(node_ids)
            frames = lax.dynamic_slice_in_dim(frames_pad, first_node, SPAN_MOST, 0)
            centre_win = lax.dynamic_slice_in_dim(centre_pad, first_node, SPAN_MOST, 0)
            return (add_window(carry, first_node, local_moment(block, member, frames, centre_win)), None)
        moments, _ = lax.scan(sweep_block, jnp.zeros((padded, width, AXES), jnp.float32), (blocks, id_blocks))
        frames = jax.vmap(orthonormal)(moments[:NODES])
        frames_pad = jnp.concatenate([frames, jnp.zeros((SPAN_MOST, width, AXES), jnp.float32)], 0)

    def final_block(carry, item):
        block, node_ids = item
        first_node, member = window_member(node_ids)
        frames = lax.dynamic_slice_in_dim(frames_pad, first_node, SPAN_MOST, 0)
        centre_win = lax.dynamic_slice_in_dim(centre_pad, first_node, SPAN_MOST, 0)
        terms = lifted_terms(block, frames, centre_win)
        return (carry, lax.optimization_barrier(jnp.sum(terms * member[:, :, None], 1)))
    _, coords = lax.scan(final_block, jnp.float32(0.0), (blocks, id_blocks))
    return coords.reshape(TOTAL, AXES).T
```

```python
import functools

import jax
import jax.numpy as jnp
from jax import lax
from jax.experimental import pallas as pl
from jax.experimental.pallas import tpu as pltpu
from jax.sharding import PartitionSpec as P

ITERS = 3
SLOTS = 8
LANES = 128
BLOCK = 1024
F32 = jnp.float32
BF16 = jnp.bfloat16
MIB = 1 << 20


def dot_nt(a, b):
    return lax.dot_general(a, b, (((1,), (1,)), ((), ())), preferred_element_type=F32)


def dot_nn(a, b):
    return lax.dot_general(a, b, (((1,), (0,)), ((), ())), preferred_element_type=F32)


def fold_lanes(value):
    total = value[:, :LANES]
    for start in range(LANES, value.shape[1], LANES):
        total = total + value[:, start : start + LANES]
    return total


def same(a, b):
    return jnp.where(a == b, 1.0, 0.0).astype(F32)


def put_rows(tall_ref, value, at, flat):
    size = value.shape[0]
    for tile in range(value.shape[1] // LANES):
        tall_ref[pl.ds(tile * flat + at, size), :] = value[:, tile * LANES : (tile + 1) * LANES]


def put_strided(tall_ref, value, index, axes):
    flat = SLOTS * axes
    for tile in range(value.shape[1] // LANES):
        tall_ref[pl.ds(tile * flat + index, SLOTS, stride=axes), :] = value[
            :, tile * LANES : (tile + 1) * LANES
        ]


def get_strided(tall_ref, index, axes):
    flat = SLOTS * axes
    tiles = tall_ref.shape[0] // flat
    return jnp.concatenate(
        [tall_ref[pl.ds(tile * flat + index, SLOTS, stride=axes), :] for tile in range(tiles)], 1
    )


def get_flat(tall_ref, flat):
    tiles = tall_ref.shape[0] // flat
    return jnp.concatenate([tall_ref[tile * flat : (tile + 1) * flat, :] for tile in range(tiles)], 1)


def ends_of(nodes_ref):
    nodes = nodes_ref[...]
    return jnp.min(nodes), jnp.max(nodes)


def first_sweep_kernel(axes, points_ref, nodes_ref, init_ref, part_ref, sums_ref, note_ref):
    rows, width = points_ref.shape
    first, last = ends_of(nodes_ref)
    frame = init_ref[...].T.astype(BF16)
    slot_rows = SLOTS * axes
    moment = jnp.zeros((2 * slot_rows + SLOTS, width), F32)
    columns = jnp.zeros((slot_rows, LANES), F32)
    counts = jnp.zeros((SLOTS, LANES), F32)
    for start in range(0, rows, BLOCK):
        block = points_ref[start : start + BLOCK, :]
        slot_of = nodes_ref[:, start : start + BLOCK] - first
        spread = dot_nt(frame, block)
        high = spread.astype(BF16).astype(F32)
        low = (spread - high).astype(BF16).astype(F32)
        highs = []
        lows = []
        for slot in range(SLOTS):
            here = slot_of == slot
            highs.append(jnp.where(here, high, 0.0))
            lows.append(jnp.where(here, low, 0.0))
        highs = jnp.concatenate(highs, 0)
        lows = jnp.concatenate(lows, 0)
        member = (slot_of == lax.broadcasted_iota(jnp.int32, (SLOTS, BLOCK), 0)).astype(F32)
        left = jnp.concatenate([highs.astype(BF16), lows.astype(BF16), member.astype(BF16)], 0)
        moment = moment + dot_nn(left, block)
        columns = columns + fold_lanes(highs + lows)
        counts = counts + fold_lanes(member)
    part_ref[:, :width] = moment[:slot_rows] + moment[slot_rows : 2 * slot_rows]
    part_ref[:, width:] = jnp.broadcast_to(jnp.sum(columns, 1, keepdims=True), columns.shape)
    sums_ref[:, :width] = moment[2 * slot_rows :]
    sums_ref[:, width:] = jnp.broadcast_to(jnp.sum(counts, 1, keepdims=True), counts.shape)
    span = last - first
    tail = pl.multiple_of(span * axes, axes)
    note_ref[:axes, :] = part_ref[:axes, :]
    note_ref[axes : 2 * axes, :] = part_ref[pl.ds(tail, axes), :]
    base = 2 * axes
    wide = sums_ref.shape[1]
    note_ref[base : base + 1, :] = sums_ref[0:1, :]
    note_ref[base + 1 : base + 2, :] = sums_ref[pl.ds(span, 1), :]
    note_ref[base + 2 : base + 3, :] = jnp.full((1, wide), first.astype(F32))
    note_ref[base + 3 : base + 4, :] = jnp.full((1, wide), last.astype(F32))
    note_ref[base + 4 :, :] = jnp.zeros((4, wide), F32)


def weigh(axes, own, groups):
    base = 2 * axes
    first = own[base + 2 : base + 3, :1]
    last = own[base + 3 : base + 4, :1]
    heads = [g[base + 2 : base + 3, :1] for g in groups]
    tails = [g[base + 3 : base + 4, :1] for g in groups]
    lowest = functools.reduce(jnp.minimum, heads)
    highest = functools.reduce(jnp.maximum, tails)
    weights = []
    for index, (head, tail) in enumerate(zip(heads, tails)):
        other = 0.0 if index == 0 else 1.0
        weights.append(
            (
                same(head, lowest),
                same(tail, highest),
                other * same(head, first) * (1.0 - same(tail, first)),
                other * same(tail, first),
                other * same(head, last),
                other * same(tail, last) * (1.0 - same(head, last)),
            )
        )
    return weights, lowest, highest


def store_weights(weight_ref, weights):
    flat = [w for source in weights for w in source]
    weight_ref[...] = jnp.zeros(weight_ref.shape, F32)
    for index, weight in enumerate(flat):
        weight_ref[index : index + 1, :] = jnp.broadcast_to(weight, (1, LANES))


def load_weights(weight_ref, count):
    flat = [weight_ref[index : index + 1, :1] for index in range(6 * count)]
    return [tuple(flat[6 * k : 6 * k + 6]) for k in range(count)]


def join_own(own_head, own_tail, pairs, weights):
    head, tail = own_head, own_tail
    for (group_head, group_tail), w in zip(pairs[1:], weights[1:]):
        head = head + w[2] * group_head + w[3] * group_tail
        tail = tail + w[4] * group_head + w[5] * group_tail
    return head, tail


def join_group(pairs, weights):
    head = sum(w[0] * pair[0] for pair, w in zip(pairs, weights))
    tail = sum(w[1] * pair[1] for pair, w in zip(pairs, weights))
    return head, tail


def pairs_of(axes, notes):
    return [(note[:axes, :], note[axes : 2 * axes, :]) for note in notes]


def sum_pairs_of(axes, notes):
    base = 2 * axes
    return [(note[base : base + 1, :], note[base + 1 : base + 2, :]) for note in notes]


def first_join_kernel(axes, count, own_ref, *refs):
    groups = refs[:count]
    own_out, group_out, weight_ref = refs[count:]
    weights, lowest, highest = weigh(axes, own_ref, groups)
    store_weights(weight_ref, weights)
    base = 2 * axes
    wide = own_ref.shape[1]
    own_out[base:, :] = own_ref[base:, :]
    group_out[base:, :] = jnp.zeros((8, wide), F32)
    group_out[base + 2 : base + 3, :] = jnp.broadcast_to(lowest, (1, wide))
    group_out[base + 3 : base + 4, :] = jnp.broadcast_to(highest, (1, wide))
    for pairs, at, size in (
        (pairs_of(axes, groups), 0, axes),
        (sum_pairs_of(axes, groups), base, 1),
    ):
        head, tail = join_own(
            own_ref[at : at + size, :], own_ref[at + size : at + 2 * size, :], pairs, weights
        )
        own_out[at : at + size, :] = head
        own_out[at + size : at + 2 * size, :] = tail
        head, tail = join_group(pairs, weights)
        group_out[at : at + size, :] = head
        group_out[at + size : at + 2 * size, :] = tail


def join_kernel(axes, count, own_ref, weight_ref, *refs):
    groups = refs[:count]
    own_out, group_out = refs[count:]
    weights = load_weights(weight_ref, count)
    pairs = pairs_of(axes, groups)
    head, tail = join_own(own_ref[:axes, :], own_ref[axes:, :], pairs, weights)
    own_out[:axes, :] = head
    own_out[axes:, :] = tail
    head, tail = join_group(pairs, weights)
    group_out[:axes, :] = head
    group_out[axes:, :] = tail


def find_frames(axes, columns, centre, live, flat_ref, offset_ref):
    found = list(columns)
    for index in range(axes):
        lead = found[index]
        length = jnp.sum(lead * lead, 1, keepdims=True)
        length = jnp.where(live, length, 1.0)
        for later in range(index + 1, axes):
            share = jnp.sum(lead * found[later], 1, keepdims=True) / length
            found[later] = found[later] - share * lead
        unit = lead / jnp.sqrt(length)
        put_strided(flat_ref, unit, index, axes)
        offset = jnp.sum(centre * unit, 1, keepdims=True)
        put_strided(offset_ref, jnp.broadcast_to(offset, (SLOTS, LANES)), index, axes)


def sweep_blocks(axes, points_ref, nodes_ref, first, flat_ref, offset_ref):
    rows, width = points_ref.shape
    frames = get_flat(flat_ref, SLOTS * axes).astype(BF16)
    offset = offset_ref[:, :1]
    moment = jnp.zeros((SLOTS * axes, width), F32)
    columns = jnp.zeros((SLOTS * axes, LANES), F32)
    for start in range(0, rows, BLOCK):
        block = points_ref[start : start + BLOCK, :]
        slot_of = nodes_ref[:, start : start + BLOCK] - first
        terms = dot_nt(frames, block) - offset
        kept = [
            jnp.where(slot_of == slot, terms[slot * axes : (slot + 1) * axes], 0.0)
            for slot in range(SLOTS)
        ]
        lifted = jnp.concatenate(kept, 0).astype(BF16)
        moment = moment + dot_nn(lifted, block)
        columns = columns + fold_lanes(lifted.astype(F32))
    return moment, jnp.sum(columns, 1, keepdims=True)


def project_blocks(axes, points_ref, nodes_ref, first, flat_ref, offset_ref, out_ref):
    rows = points_ref.shape[0]
    frames = get_flat(flat_ref, SLOTS * axes).astype(BF16)
    offset = offset_ref[:, :1]
    for start in range(0, rows, BLOCK):
        block = points_ref[start : start + BLOCK, :]
        slot_of = nodes_ref[:, start : start + BLOCK] - first
        terms = dot_nt(frames, block) - offset
        out_ref[:, start : start + BLOCK] = sum(
            jnp.where(slot_of == slot, terms[slot * axes : (slot + 1) * axes], 0.0)
            for slot in range(SLOTS)
        )


def emit_part(axes, moment, column_sums, centre, span, part_ref, note_ref):
    for slot in range(SLOTS):
        at = slice(slot * axes, (slot + 1) * axes)
        part_ref[at, :] = moment[at] - column_sums[at] * centre[slot : slot + 1, :]
    tail = pl.multiple_of(span * axes, axes)
    note_ref[:axes, :] = part_ref[:axes, :]
    note_ref[axes:, :] = part_ref[pl.ds(tail, axes), :]


def live_slots(span):
    return lax.broadcasted_iota(jnp.int32, (SLOTS, 1), 0) <= span


def second_sweep_kernel(axes, count, points_ref, nodes_ref, part_ref, sums_ref, own_ref, *refs):
    groups = refs[:count]
    part_out, note_out, centre_ref, weight_ref, flat_ref, offset_ref, whole_ref, total_ref = refs[count:]
    width = points_ref.shape[1]
    first, last = ends_of(nodes_ref)
    span = last - first
    weights, _, _ = weigh(axes, own_ref, groups)
    store_weights(weight_ref, weights)
    base = 2 * axes
    head, tail = join_own(
        own_ref[:axes, :], own_ref[axes:base, :], pairs_of(axes, groups), weights
    )
    flat = SLOTS * axes
    put_rows(whole_ref, part_ref[...], 0, flat)
    put_rows(whole_ref, tail, pl.multiple_of(span * axes, axes), flat)
    put_rows(whole_ref, head, 0, flat)
    head, tail = join_own(
        own_ref[base : base + 1, :], own_ref[base + 1 : base + 2, :], sum_pairs_of(axes, groups), weights
    )
    total_ref[...] = sums_ref[...]
    total_ref[pl.ds(span, 1), :] = tail
    total_ref[:1, :] = head
    live = live_slots(span)
    counts = jnp.where(live, total_ref[:, width : width + 1], 1.0)
    centre = total_ref[:, :width] / counts
    centre_ref[...] = centre
    columns = []
    for index in range(axes):
        column = get_strided(whole_ref, index, axes)
        columns.append(column[:, :width] - column[:, width : width + 1] * centre)
    find_frames(axes, columns, centre, live, flat_ref, offset_ref)
    moment, column_sums = sweep_blocks(axes, points_ref, nodes_ref, first, flat_ref, offset_ref)
    emit_part(axes, moment, column_sums, centre_ref[...], span, part_out, note_out)


def settle_frames(axes, nodes_ref, part_ref, centre_ref, own_ref, weight_ref, groups, flat_ref, offset_ref, whole_ref):
    first, last = ends_of(nodes_ref)
    span = last - first
    weights = load_weights(weight_ref, len(groups))
    head, tail = join_own(own_ref[:axes, :], own_ref[axes:, :], pairs_of(axes, groups), weights)
    flat = SLOTS * axes
    put_rows(whole_ref, part_ref[...], 0, flat)
    put_rows(whole_ref, tail, pl.multiple_of(span * axes, axes), flat)
    put_rows(whole_ref, head, 0, flat)
    columns = [get_strided(whole_ref, index, axes) for index in range(axes)]
    find_frames(axes, columns, centre_ref[...], live_slots(span), flat_ref, offset_ref)
    return first, span


def sweep_kernel(axes, count, points_ref, nodes_ref, part_ref, centre_ref, own_ref, weight_ref, *refs):
    groups = refs[:count]
    part_out, note_out, flat_ref, offset_ref, whole_ref = refs[count:]
    first, span = settle_frames(
        axes, nodes_ref, part_ref, centre_ref, own_ref, weight_ref, groups, flat_ref, offset_ref, whole_ref
    )
    moment, column_sums = sweep_blocks(axes, points_ref, nodes_ref, first, flat_ref, offset_ref)
    emit_part(axes, moment, column_sums, centre_ref[...], span, part_out, note_out)


def project_kernel(axes, count, points_ref, nodes_ref, part_ref, centre_ref, own_ref, weight_ref, *refs):
    groups = refs[:count]
    out_ref, flat_ref, offset_ref, whole_ref = refs[count:]
    first, _ = settle_frames(
        axes, nodes_ref, part_ref, centre_ref, own_ref, weight_ref, groups, flat_ref, offset_ref, whole_ref
    )
    project_blocks(axes, points_ref, nodes_ref, first, flat_ref, offset_ref, out_ref)


def radices(size):
    found = []
    while size % 4 == 0:
        found.append(4)
        size //= 4
    factor = 2
    while size > 1:
        while size % factor == 0:
            found.insert(0, factor)
            size //= factor
        factor += 1
    return found


def stages_of(mesh):
    stages = []
    stride = 1
    for name in ("col", "row"):
        for radix in radices(mesh.shape[name]):
            stages.append((stride, radix))
            stride *= radix
    return stages


def swap(value, stage, devices):
    stride, radix = stage
    groups = [value]
    for shift in range(1, radix):
        pairs = []
        for source in range(devices):
            place = source // stride % radix
            target = source + ((place + shift) % radix - place) * stride
            pairs.append((source, target))
        groups.append(lax.ppermute(value, ("row", "col"), pairs))
    return groups


def shape(*dims):
    return jax.ShapeDtypeStruct(dims, F32)


def call(kernel, outs, scratch=(), limit=8):
    vmem = pl.BlockSpec(memory_space=pltpu.VMEM)

    def run(*args):
        return pl.pallas_call(
            kernel,
            out_shape=outs,
            in_specs=[vmem] * len(args),
            out_specs=jax.tree.map(lambda _: vmem, outs),
            scratch_shapes=scratch,
            compiler_params=pltpu.CompilerParams(vmem_limit_bytes=limit * MIB),
        )(*args)

    return run


def solution(mesh):
    stages = stages_of(mesh)
    devices = mesh.shape["row"] * mesh.shape["col"]

    def shards(points, node_of_row, init_axes):
        rows, width = points.shape
        axes = init_axes.shape[1]
        flat = SLOTS * axes
        wide = width + LANES
        nodes = node_of_row.reshape(1, rows)
        note_rows = 2 * axes + 8
        tall = flat * width // LANES
        frame_scratch = [pltpu.VMEM((tall, LANES), F32), pltpu.VMEM((flat, LANES), F32)]
        part, sums, note = call(
            functools.partial(first_sweep_kernel, axes),
            (shape(flat, wide), shape(SLOTS, wide), shape(note_rows, wide)),
            limit=32,
        )(points, nodes, init_axes)
        own = group = note
        kept = []
        for stage in stages[:-1]:
            groups = swap(group, stage, devices)
            count = len(groups)
            own, group, weight = call(
                functools.partial(first_join_kernel, axes, count),
                (shape(note_rows, wide), shape(note_rows, wide), shape(8 * count, LANES)),
            )(own, *groups)
            kept.append(weight)
        groups = swap(group, stages[-1], devices)
        count = len(groups)
        part, note, centre, weight = call(
            functools.partial(second_sweep_kernel, axes, count),
            (shape(flat, width), shape(2 * axes, width), shape(SLOTS, width), shape(8 * count, LANES)),
            frame_scratch + [pltpu.VMEM((tall + flat, LANES), F32), pltpu.VMEM((SLOTS, wide), F32)],
            limit=32,
        )(points, nodes, part, sums, own, *groups)
        kept.append(weight)
        for repeat in range(1, ITERS):
            own = group = note
            for stage, weight in zip(stages[:-1], kept):
                groups = swap(group, stage, devices)
                own, group = call(
                    functools.partial(join_kernel, axes, len(groups)),
                    (shape(2 * axes, width), shape(2 * axes, width)),
                )(own, weight, *groups)
            groups = swap(group, stages[-1], devices)
            if repeat < ITERS - 1:
                part, note = call(
                    functools.partial(sweep_kernel, axes, len(groups)),
                    (shape(flat, width), shape(2 * axes, width)),
                    frame_scratch + [pltpu.VMEM((tall, LANES), F32)],
                    limit=32,
                )(points, nodes, part, centre, own, kept[-1], *groups)
        return call(
            functools.partial(project_kernel, axes, len(groups)),
            shape(axes, rows),
            frame_scratch + [pltpu.VMEM((tall, LANES), F32)],
            limit=32,
        )(points, nodes, part, centre, own, kept[-1], *groups)

    in_specs = (P(("row", "col"), None), P(("row", "col")), P())
    out_specs = P(None, ("row", "col"))
    return jax.shard_map(shards, mesh=mesh, in_specs=in_specs, out_specs=out_specs, check_vma=False)
```

```python
import functools

import jax
import jax.numpy as jnp
from jax import lax
from jax.experimental import pallas as pl
from jax.experimental.pallas import tpu as pltpu
from jax.sharding import PartitionSpec as P

ITERS = 3
SLOTS = 8
LANES = 128
BLOCK = 2048
PIECE = 1024
AHEAD = 3
FIRST = 1024
STEP = 2048
F32 = jnp.float32
BF16 = jnp.bfloat16
MIB = 1 << 20


def dot_nt(a, b):
    return lax.dot_general(a, b, (((1,), (1,)), ((), ())), preferred_element_type=F32)


def dot_nn(a, b):
    return lax.dot_general(a, b, (((1,), (0,)), ((), ())), preferred_element_type=F32)


def fold_lanes(value):
    total = value[:, :LANES]
    for start in range(LANES, value.shape[1], LANES):
        total = total + value[:, start : start + LANES]
    return total


def same(a, b):
    return jnp.where(a == b, 1.0, 0.0).astype(F32)


def put_rows(tall_ref, value, at, flat):
    size = value.shape[0]
    for tile in range(value.shape[1] // LANES):
        tall_ref[pl.ds(tile * flat + at, size), :] = value[:, tile * LANES : (tile + 1) * LANES]


def put_strided(tall_ref, value, index, axes):
    flat = SLOTS * axes
    for tile in range(value.shape[1] // LANES):
        tall_ref[pl.ds(tile * flat + index, SLOTS, stride=axes), :] = value[
            :, tile * LANES : (tile + 1) * LANES
        ]


def get_strided(tall_ref, index, axes):
    flat = SLOTS * axes
    tiles = tall_ref.shape[0] // flat
    return jnp.concatenate(
        [tall_ref[pl.ds(tile * flat + index, SLOTS, stride=axes), :] for tile in range(tiles)], 1
    )


def get_flat(tall_ref, flat):
    tiles = tall_ref.shape[0] // flat
    return jnp.concatenate([tall_ref[tile * flat : (tile + 1) * flat, :] for tile in range(tiles)], 1)


def ends_of(nodes_ref):
    rows = nodes_ref.shape[1]
    return jnp.min(nodes_ref[:, :LANES]), jnp.max(nodes_ref[:, rows - LANES :])


def tile_of(sums, counts, first, last):
    width = sums.shape[1]
    pieces = [sums[:, at : at + LANES] for at in range(0, width, LANES)]
    left = lax.broadcasted_iota(jnp.int32, (1, LANES), 1) < LANES // 2
    return jnp.concatenate(pieces + [counts, jnp.where(left, first, last)], 0)


def sums_of(tile, width):
    return jnp.concatenate([tile[row : row + 1] for row in range(width // LANES)], 1)


def cuts_of(rows):
    return [0] + list(range(FIRST, rows - 1, STEP)) + [rows]


def first_sweep_kernel(axes, points_hbm, nodes_hbm, init_hbm, part_ref, sums_ref, note_ref, points_ref, nodes_ref, init_ref, sems):
    rows, width = points_ref.shape
    small = [
        pltpu.make_async_copy(nodes_hbm, nodes_ref, sems.at[0]),
        pltpu.make_async_copy(init_hbm, init_ref, sems.at[1]),
    ]
    cuts = cuts_of(rows)
    copies = []
    for start, stop in zip(cuts[:-1], cuts[1:]):
        at = pl.ds(start, stop - start)
        sem = sems.at[2 + len(copies)]
        copies.append(pltpu.make_async_copy(points_hbm.at[at], points_ref.at[at], sem))
    for copy in small + copies[:AHEAD]:
        copy.start()
    for copy in small:
        copy.wait()
    first, last = ends_of(nodes_ref)
    frame = init_ref[...].astype(BF16)
    slot_rows = SLOTS * axes
    moment = jnp.zeros((2 * slot_rows + SLOTS, width), F32)
    counts = jnp.zeros((SLOTS, LANES), F32)
    left = block = None
    for start in range(0, rows, PIECE):
        if start in cuts:
            piece = cuts.index(start)
            copies[piece].wait()
            if piece + AHEAD < len(copies):
                copies[piece + AHEAD].start()
        before, left_before = block, left
        block = points_ref[start : start + PIECE, :]
        spread = dot_nt(frame, block)
        if start > 0:
            moment = moment + dot_nn(left_before, before)
        slot_of = nodes_ref[:, start : start + PIECE] - first
        high = spread.astype(BF16).astype(F32)
        low = spread - high
        highs = []
        lows = []
        for slot in range(SLOTS):
            here = slot_of == slot
            highs.append(jnp.where(here, high, 0.0))
            lows.append(jnp.where(here, low, 0.0))
        member = (slot_of == lax.broadcasted_iota(jnp.int32, (SLOTS, PIECE), 0)).astype(F32)
        left = jnp.concatenate(highs + lows + [member], 0).astype(BF16)
        counts = counts + fold_lanes(member)
    moment = moment + dot_nn(left, block)
    part_ref[...] = moment[:slot_rows] + moment[slot_rows : 2 * slot_rows]
    sums_ref[:, :width] = moment[2 * slot_rows :]
    sums_ref[:, width:] = jnp.broadcast_to(jnp.sum(counts, 1, keepdims=True), counts.shape)
    span = last - first
    ids = (first.astype(F32), last.astype(F32))
    for at, slot in ((0, 0), (axes, span)):
        own = sums_ref[pl.ds(slot, 1), :]
        note_ref[at : at + axes, :width] = part_ref[pl.ds(pl.multiple_of(slot * axes, axes), axes), :]
        note_ref[at : at + axes, width:] = tile_of(own[:, :width], own[:, width:], *ids)


def weigh(axes, own, groups):
    width = own.shape[1] - LANES
    half = width + LANES // 2
    first = own[axes - 1 : axes, width : width + 1]
    last = own[axes - 1 : axes, half : half + 1]
    heads = [g[axes - 1 : axes, width : width + 1] for g in groups]
    tails = [g[axes - 1 : axes, half : half + 1] for g in groups]
    lowest = functools.reduce(jnp.minimum, heads)
    highest = functools.reduce(jnp.maximum, tails)
    weights = []
    for index, (head, tail) in enumerate(zip(heads, tails)):
        other = 0.0 if index == 0 else 1.0
        weights.append(
            (
                same(head, lowest),
                same(tail, highest),
                other * same(head, first) * (1.0 - same(tail, first)),
                other * same(tail, first),
                other * same(head, last),
                other * same(tail, last) * (1.0 - same(head, last)),
            )
        )
    return weights, lowest, highest


def store_weights(weight_ref, weights):
    flat = [w for source in weights for w in source]
    weight_ref[...] = jnp.zeros(weight_ref.shape, F32)
    for index, weight in enumerate(flat):
        weight_ref[index : index + 1, :] = jnp.broadcast_to(weight, (1, LANES))


def load_weights(weight_ref, count):
    flat = [weight_ref[index : index + 1, :1] for index in range(6 * count)]
    return [tuple(flat[6 * k : 6 * k + 6]) for k in range(count)]


def join_own(axes, own, groups, weights):
    head, tail = own[:axes, :], own[axes:, :]
    for group, w in zip(groups[1:], weights[1:]):
        group_head, group_tail = group[:axes, :], group[axes:, :]
        head = head + w[2] * group_head + w[3] * group_tail
        tail = tail + w[4] * group_head + w[5] * group_tail
    return head, tail


def join_group(axes, groups, weights):
    head = sum(w[0] * group[:axes, :] for group, w in zip(groups, weights))
    tail = sum(w[1] * group[axes:, :] for group, w in zip(groups, weights))
    return head, tail


def mark(ref, axes, first, last):
    width = ref.shape[1] - LANES
    left = lax.broadcasted_iota(jnp.int32, (1, LANES), 1) < LANES // 2
    for row in (axes - 1, 2 * axes - 1):
        ref[row : row + 1, width:] = jnp.where(left, first, last)


def first_join_kernel(axes, count, own_ref, *refs):
    groups = refs[:count]
    own_out, group_out, weight_ref = refs[count:]
    width = own_ref.shape[1] - LANES
    half = width + LANES // 2
    weights, lowest, highest = weigh(axes, own_ref, groups)
    store_weights(weight_ref, weights)
    own_out[:axes, :], own_out[axes:, :] = join_own(axes, own_ref, groups, weights)
    group_out[:axes, :], group_out[axes:, :] = join_group(axes, groups, weights)
    mark(own_out, axes, own_ref[axes - 1 : axes, width : width + 1], own_ref[axes - 1 : axes, half : half + 1])
    mark(group_out, axes, lowest, highest)


def join_kernel(axes, count, own_ref, weight_ref, *refs):
    groups = refs[:count]
    own_out, group_out = refs[count:]
    weights = load_weights(weight_ref, count)
    own_out[:axes, :], own_out[axes:, :] = join_own(axes, own_ref, groups, weights)
    group_out[:axes, :], group_out[axes:, :] = join_group(axes, groups, weights)


def find_frames(axes, columns, centre, live, flat_ref, offset_ref):
    found = list(columns)
    for index in range(axes):
        lead = found[index]
        length = jnp.sum(lead * lead, 1, keepdims=True)
        length = jnp.where(live, length, 1.0)
        for later in range(index + 1, axes):
            share = jnp.sum(lead * found[later], 1, keepdims=True) / length
            found[later] = found[later] - share * lead
        unit = lead / jnp.sqrt(length)
        put_strided(flat_ref, unit, index, axes)
        offset = jnp.sum(centre * unit, 1, keepdims=True)
        put_strided(offset_ref, jnp.broadcast_to(offset, (SLOTS, LANES)), index, axes)


def sweep_blocks(axes, points_ref, nodes_ref, first, flat_ref, offset_ref):
    rows, width = points_ref.shape
    frames = get_flat(flat_ref, SLOTS * axes).astype(BF16)
    offset = offset_ref[:, :1]
    moment = jnp.zeros((SLOTS * axes, width), F32)
    columns = jnp.zeros((SLOTS * axes, LANES), F32)
    for start in range(0, rows, BLOCK):
        block = points_ref[start : start + BLOCK, :]
        slot_of = nodes_ref[:, start : start + BLOCK] - first
        terms = dot_nt(frames, block) - offset
        kept = [
            jnp.where(slot_of == slot, terms[slot * axes : (slot + 1) * axes], 0.0)
            for slot in range(SLOTS)
        ]
        lifted = jnp.concatenate(kept, 0).astype(BF16)
        moment = moment + dot_nn(lifted, block)
        columns = columns + fold_lanes(lifted.astype(F32))
    return moment, jnp.sum(columns, 1, keepdims=True)


def project_blocks(axes, points_ref, nodes_ref, first, flat_ref, offset_ref, out_ref):
    rows = points_ref.shape[0]
    frames = get_flat(flat_ref, SLOTS * axes).astype(BF16)
    offset = offset_ref[:, :1]
    for start in range(0, rows, BLOCK):
        block = points_ref[start : start + BLOCK, :]
        slot_of = nodes_ref[:, start : start + BLOCK] - first
        terms = dot_nt(frames, block) - offset
        out_ref[:, start : start + BLOCK] = sum(
            jnp.where(slot_of == slot, terms[slot * axes : (slot + 1) * axes], 0.0)
            for slot in range(SLOTS)
        )


def emit_part(axes, moment, column_sums, centre, span, part_ref, note_ref):
    for slot in range(SLOTS):
        at = slice(slot * axes, (slot + 1) * axes)
        part_ref[at, :] = moment[at] - column_sums[at] * centre[slot : slot + 1, :]
    tail = pl.multiple_of(span * axes, axes)
    note_ref[:axes, :] = part_ref[:axes, :]
    note_ref[axes:, :] = part_ref[pl.ds(tail, axes), :]


def live_slots(span):
    return lax.broadcasted_iota(jnp.int32, (SLOTS, 1), 0) <= span


def second_sweep_kernel(axes, count, points_ref, nodes_ref, init_ref, part_ref, sums_ref, own_ref, *refs):
    groups = refs[:count]
    part_out, note_out, centre_ref, weight_ref, flat_ref, offset_ref, whole_ref = refs[count:]
    width = points_ref.shape[1]
    first, last = ends_of(nodes_ref)
    span = last - first
    weights, _, _ = weigh(axes, own_ref, groups)
    store_weights(weight_ref, weights)
    head, tail = join_own(axes, own_ref, groups, weights)
    flat = SLOTS * axes
    put_rows(whole_ref, part_ref[...], 0, flat)
    put_rows(whole_ref, tail[:, :width], pl.multiple_of(span * axes, axes), flat)
    put_rows(whole_ref, head[:, :width], 0, flat)
    counted = width // LANES
    slots = lax.broadcasted_iota(jnp.int32, (SLOTS, 1), 0)
    sums = sums_ref[:, :width]
    counts = sums_ref[:, width:]
    for slot, tile in ((span, tail[:, width:]), (0, head[:, width:])):
        sums = jnp.where(slots == slot, sums_of(tile, width), sums)
        counts = jnp.where(slots == slot, tile[counted : counted + 1], counts)
    live = live_slots(span)
    centre = sums / jnp.where(live, counts[:, :1], 1.0)
    centre_ref[...] = centre
    start = init_ref[...].astype(BF16).astype(F32)
    columns = []
    for index in range(axes):
        spread = jnp.sum(sums * start[index : index + 1], 1, keepdims=True)
        columns.append(get_strided(whole_ref, index, axes) - spread * centre)
    find_frames(axes, columns, centre, live, flat_ref, offset_ref)
    moment, column_sums = sweep_blocks(axes, points_ref, nodes_ref, first, flat_ref, offset_ref)
    emit_part(axes, moment, column_sums, centre_ref[...], span, part_out, note_out)


def settle_frames(axes, nodes_ref, part_ref, centre_ref, own_ref, weight_ref, groups, flat_ref, offset_ref, whole_ref):
    first, last = ends_of(nodes_ref)
    span = last - first
    weights = load_weights(weight_ref, len(groups))
    head, tail = join_own(axes, own_ref, groups, weights)
    flat = SLOTS * axes
    put_rows(whole_ref, part_ref[...], 0, flat)
    put_rows(whole_ref, tail, pl.multiple_of(span * axes, axes), flat)
    put_rows(whole_ref, head, 0, flat)
    columns = [get_strided(whole_ref, index, axes) for index in range(axes)]
    find_frames(axes, columns, centre_ref[...], live_slots(span), flat_ref, offset_ref)
    return first, span


def sweep_kernel(axes, count, points_ref, nodes_ref, part_ref, centre_ref, own_ref, weight_ref, *refs):
    groups = refs[:count]
    part_out, note_out, flat_ref, offset_ref, whole_ref = refs[count:]
    first, span = settle_frames(
        axes, nodes_ref, part_ref, centre_ref, own_ref, weight_ref, groups, flat_ref, offset_ref, whole_ref
    )
    moment, column_sums = sweep_blocks(axes, points_ref, nodes_ref, first, flat_ref, offset_ref)
    emit_part(axes, moment, column_sums, centre_ref[...], span, part_out, note_out)


def project_kernel(axes, count, points_ref, nodes_ref, part_ref, centre_ref, own_ref, weight_ref, *refs):
    groups = refs[:count]
    out_ref, flat_ref, offset_ref, whole_ref = refs[count:]
    first, _ = settle_frames(
        axes, nodes_ref, part_ref, centre_ref, own_ref, weight_ref, groups, flat_ref, offset_ref, whole_ref
    )
    project_blocks(axes, points_ref, nodes_ref, first, flat_ref, offset_ref, out_ref)


def radices(size):
    found = []
    while size % 4 == 0:
        found.append(4)
        size //= 4
    factor = 2
    while size > 1:
        while size % factor == 0:
            found.insert(0, factor)
            size //= factor
        factor += 1
    return found


def stages_of(mesh):
    stages = []
    stride = 1
    for name in ("col", "row"):
        for radix in radices(mesh.shape[name]):
            stages.append((stride, radix))
            stride *= radix
    return stages


def swap(value, stage, devices):
    stride, radix = stage
    groups = [value]
    for shift in range(1, radix):
        pairs = []
        for source in range(devices):
            place = source // stride % radix
            other = place ^ shift if radix & (radix - 1) == 0 else (place + shift) % radix
            target = source + (other - place) * stride
            pairs.append((source, target))
        groups.append(lax.ppermute(value, ("row", "col"), pairs))
    return groups


def shape(*dims):
    return jax.ShapeDtypeStruct(dims, F32)


def call(kernel, outs, scratch=(), limit=8, source=pltpu.VMEM):
    vmem = pl.BlockSpec(memory_space=pltpu.VMEM)

    def run(*args):
        return pl.pallas_call(
            kernel,
            out_shape=outs,
            in_specs=[pl.BlockSpec(memory_space=source)] * len(args),
            out_specs=jax.tree.map(lambda _: vmem, outs),
            scratch_shapes=scratch,
            compiler_params=pltpu.CompilerParams(vmem_limit_bytes=limit * MIB),
        )(*args)

    return run


def solution(mesh):
    stages = stages_of(mesh)
    devices = mesh.shape["row"] * mesh.shape["col"]

    def shards(points, node_of_row, init_axes):
        rows, width = points.shape
        axes = init_axes.shape[1]
        flat = SLOTS * axes
        wide = width + LANES
        tall = flat * width // LANES
        frame_scratch = [pltpu.VMEM((tall, LANES), F32), pltpu.VMEM((flat, LANES), F32)]
        part, sums, note, points, nodes, init = call(
            functools.partial(first_sweep_kernel, axes),
            (
                shape(flat, width),
                shape(SLOTS, wide),
                shape(2 * axes, wide),
                jax.ShapeDtypeStruct((rows, width), points.dtype),
                jax.ShapeDtypeStruct((1, rows), node_of_row.dtype),
                shape(axes, width),
            ),
            [pltpu.SemaphoreType.DMA((len(cuts_of(rows)) + 1,))],
            limit=32,
            source=pltpu.HBM,
        )(*[pltpu.with_memory_space_constraint(each, pltpu.HBM) for each in (points, node_of_row.reshape(1, rows), init_axes.T)])
        own = group = note
        kept = []
        for stage in stages[:-1]:
            groups = swap(group, stage, devices)
            count = len(groups)
            own, group, weight = call(
                functools.partial(first_join_kernel, axes, count),
                (shape(2 * axes, wide), shape(2 * axes, wide), shape(8 * count, LANES)),
            )(own, *groups)
            kept.append(weight)
        groups = swap(group, stages[-1], devices)
        count = len(groups)
        part, note, centre, weight = call(
            functools.partial(second_sweep_kernel, axes, count),
            (shape(flat, width), shape(2 * axes, width), shape(SLOTS, width), shape(8 * count, LANES)),
            frame_scratch + [pltpu.VMEM((tall, LANES), F32)],
            limit=32,
        )(points, nodes, init, part, sums, own, *groups)
        kept.append(weight)
        for repeat in range(1, ITERS):
            own = group = note
            for stage, weight in zip(stages[:-1], kept):
                groups = swap(group, stage, devices)
                own, group = call(
                    functools.partial(join_kernel, axes, len(groups)),
                    (shape(2 * axes, width), shape(2 * axes, width)),
                )(own, weight, *groups)
            groups = swap(group, stages[-1], devices)
            settle = frame_scratch + [pltpu.VMEM((tall, LANES), F32)]
            if repeat < ITERS - 1:
                part, note = call(
                    functools.partial(sweep_kernel, axes, len(groups)),
                    (shape(flat, width), shape(2 * axes, width)),
                    settle,
                    limit=32,
                )(points, nodes, part, centre, own, kept[-1], *groups)
        return call(
            functools.partial(project_kernel, axes, len(groups)), shape(axes, rows), settle, limit=32
        )(points, nodes, part, centre, own, kept[-1], *groups)

    in_specs = (P(("row", "col"), None), P(("row", "col")), P())
    out_specs = P(None, ("row", "col"))
    return jax.shard_map(shards, mesh=mesh, in_specs=in_specs, out_specs=out_specs, check_vma=False)
```

```python
import functools

import jax
import jax.numpy as jnp
from jax import lax
from jax.experimental import pallas as pl
from jax.experimental.pallas import tpu as pltpu
from jax.sharding import PartitionSpec as P

ITERS = 3
SLOTS = 8
LANES = 128
BLOCK = 512
PIECE = 512
AHEAD = 3
FIRST = 2048
STEP = 2048
F32 = jnp.float32
BF16 = jnp.bfloat16
MIB = 1 << 20


def dot_nt(a, b):
    return lax.dot_general(a, b, (((1,), (1,)), ((), ())), preferred_element_type=F32)


def dot_nn(a, b):
    return lax.dot_general(a, b, (((1,), (0,)), ((), ())), preferred_element_type=F32)


def fold_lanes(value):
    total = value[:, :LANES]
    for start in range(LANES, value.shape[1], LANES):
        total = total + value[:, start : start + LANES]
    return total


def same(a, b):
    return jnp.where(a == b, 1.0, 0.0).astype(F32)


def put_rows(tall_ref, value, at, flat):
    size = value.shape[0]
    for tile in range(value.shape[1] // LANES):
        tall_ref[pl.ds(tile * flat + at, size), :] = value[:, tile * LANES : (tile + 1) * LANES]


def put_strided(tall_ref, value, index, axes):
    flat = SLOTS * axes
    for tile in range(value.shape[1] // LANES):
        tall_ref[pl.ds(tile * flat + index, SLOTS, stride=axes), :] = value[
            :, tile * LANES : (tile + 1) * LANES
        ]


def get_strided(tall_ref, index, axes):
    flat = SLOTS * axes
    tiles = tall_ref.shape[0] // flat
    return jnp.concatenate(
        [tall_ref[pl.ds(tile * flat + index, SLOTS, stride=axes), :] for tile in range(tiles)], 1
    )


def get_flat(tall_ref, flat):
    tiles = tall_ref.shape[0] // flat
    return jnp.concatenate([tall_ref[tile * flat : (tile + 1) * flat, :] for tile in range(tiles)], 1)


def ends_of(nodes_ref):
    rows = nodes_ref.shape[1]
    return jnp.min(nodes_ref[:, :LANES]), jnp.max(nodes_ref[:, rows - LANES :])


def tile_of(sums, counts, first, last):
    width = sums.shape[1]
    pieces = [sums[:, at : at + LANES] for at in range(0, width, LANES)]
    left = lax.broadcasted_iota(jnp.int32, (1, LANES), 1) < LANES // 2
    return jnp.concatenate(pieces + [counts, jnp.where(left, first, last)], 0)


def sums_of(tile, width):
    return jnp.concatenate([tile[row : row + 1] for row in range(width // LANES)], 1)


def cuts_of(rows):
    return [0] + list(range(FIRST, rows - 1, STEP)) + [rows]


def first_sweep_kernel(axes, points_hbm, nodes_hbm, init_hbm, part_ref, sums_ref, note_ref, points_ref, nodes_ref, init_ref, sems):
    rows, width = points_ref.shape
    small = [
        pltpu.make_async_copy(nodes_hbm, nodes_ref, sems.at[0]),
        pltpu.make_async_copy(init_hbm, init_ref, sems.at[1]),
    ]
    cuts = cuts_of(rows)
    copies = []
    for start, stop in zip(cuts[:-1], cuts[1:]):
        at = pl.ds(start, stop - start)
        sem = sems.at[2 + len(copies)]
        copies.append(pltpu.make_async_copy(points_hbm.at[at], points_ref.at[at], sem))
    for copy in small + copies[:AHEAD]:
        copy.start()
    for copy in small:
        copy.wait()
    first, last = ends_of(nodes_ref)
    frame = init_ref[...].astype(BF16)
    slot_rows = SLOTS * axes
    counts = jnp.zeros((SLOTS, LANES), F32)
    left = block = None
    for start in range(0, rows, PIECE):
        if start in cuts:
            piece = cuts.index(start)
            copies[piece].wait()
            if piece + AHEAD < len(copies):
                copies[piece + AHEAD].start()
        before, left_before = block, left
        block = points_ref[start : start + PIECE, :]
        spread = dot_nt(frame, block)
        if start > 0:
            product = dot_nn(left_before, before)
            part_ref[...] = product[:slot_rows] + product[slot_rows : 2 * slot_rows] + (part_ref[...] if start > PIECE else 0.0)
            sums_ref[:, :width] = product[2 * slot_rows :] + (sums_ref[:, :width] if start > PIECE else 0.0)
        slot_of = nodes_ref[:, start : start + PIECE] - first
        high = spread.astype(BF16).astype(F32)
        low = spread - high
        highs = []
        lows = []
        for slot in range(SLOTS):
            here = slot_of == slot
            highs.append(jnp.where(here, high, 0.0))
            lows.append(jnp.where(here, low, 0.0))
        member = (slot_of == lax.broadcasted_iota(jnp.int32, (SLOTS, PIECE), 0)).astype(F32)
        left = jnp.concatenate(highs + lows + [member], 0).astype(BF16)
        counts = counts + fold_lanes(member)
    product = dot_nn(left, block)
    part_ref[...] += product[:slot_rows] + product[slot_rows : 2 * slot_rows]
    sums_ref[:, :width] += product[2 * slot_rows :]
    sums_ref[:, width:] = jnp.broadcast_to(jnp.sum(counts, 1, keepdims=True), counts.shape)
    span = last - first
    ids = (first.astype(F32), last.astype(F32))
    for at, slot in ((0, 0), (axes, span)):
        own = sums_ref[pl.ds(slot, 1), :]
        note_ref[at : at + axes, :width] = part_ref[pl.ds(pl.multiple_of(slot * axes, axes), axes), :]
        note_ref[at : at + axes, width:] = tile_of(own[:, :width], own[:, width:], *ids)


def weigh(axes, own, groups):
    width = own.shape[1] - LANES
    half = width + LANES // 2
    first = own[axes - 1 : axes, width : width + 1]
    last = own[axes - 1 : axes, half : half + 1]
    heads = [g[axes - 1 : axes, width : width + 1] for g in groups]
    tails = [g[axes - 1 : axes, half : half + 1] for g in groups]
    lowest = functools.reduce(jnp.minimum, heads)
    highest = functools.reduce(jnp.maximum, tails)
    weights = []
    for index, (head, tail) in enumerate(zip(heads, tails)):
        other = 0.0 if index == 0 else 1.0
        weights.append(
            (
                same(head, lowest),
                same(tail, highest),
                other * same(head, first) * (1.0 - same(tail, first)),
                other * same(tail, first),
                other * same(head, last),
                other * same(tail, last) * (1.0 - same(head, last)),
            )
        )
    return weights, lowest, highest


def store_weights(weight_ref, weights):
    flat = [w for source in weights for w in source]
    weight_ref[...] = jnp.zeros(weight_ref.shape, F32)
    for index, weight in enumerate(flat):
        weight_ref[index : index + 1, :] = jnp.broadcast_to(weight, (1, LANES))


def load_weights(weight_ref, count, kinds=6):
    flat = [weight_ref[index : index + 1, :1] for index in range(kinds * count)]
    return [tuple(flat[kinds * k : kinds * (k + 1)]) for k in range(count)]


def join_own(axes, own, groups, weights):
    head, tail = own[:axes, :], own[axes:, :]
    for group, w in zip(groups[1:], weights[1:]):
        group_head, group_tail = group[:axes, :], group[axes:, :]
        head = head + w[2] * group_head + w[3] * group_tail
        tail = tail + w[4] * group_head + w[5] * group_tail
    return head, tail


def join_group(axes, groups, weights):
    head = sum(w[0] * group[:axes, :] for group, w in zip(groups, weights))
    tail = sum(w[1] * group[axes:, :] for group, w in zip(groups, weights))
    return head, tail


def mark(ref, axes, first, last):
    width = ref.shape[1] - LANES
    left = lax.broadcasted_iota(jnp.int32, (1, LANES), 1) < LANES // 2
    for row in range(axes - 1, ref.shape[0], axes):
        ref[row : row + 1, width:] = jnp.where(left, first, last)


def place_of(stage):
    stride, radix = stage
    index = lax.axis_index("row") * lax.axis_size("col") + lax.axis_index("col")
    return index // stride % radix


def partner(place, shift, radix):
    return place ^ shift if radix & (radix - 1) == 0 else (place + shift) % radix


def put_sends(sends, stage, head, tail):
    place = place_of(stage)
    for shift, send in enumerate(sends, 1):
        send[...] = jnp.where(partner(place, shift, stage[1]) > place, tail, head)


def first_join_kernel(axes, count, last_stage, own_ref, *refs):
    groups = refs[:count]
    own_out, weight_ref, *group_outs = refs[count:]
    width = own_ref.shape[1] - LANES
    half = width + LANES // 2
    weights, lowest, highest = weigh(axes, own_ref, groups)
    store_weights(weight_ref, weights)
    own_out[:axes, :], own_out[axes:, :] = join_own(axes, own_ref, groups, weights)
    mark(own_out, axes, own_ref[axes - 1 : axes, width : width + 1], own_ref[axes - 1 : axes, half : half + 1])
    head, tail = join_group(axes, groups, weights)
    if last_stage is None:
        group_outs[0][:axes, :] = head
        group_outs[0][axes:, :] = tail
    else:
        put_sends(group_outs, last_stage, head, tail)
    for out in group_outs:
        mark(out, axes, lowest, highest)


def join_kernel(axes, count, last_stage, own_ref, weight_ref, *refs):
    groups = refs[:count]
    own_out, *group_outs = refs[count:]
    weights = load_weights(weight_ref, count)
    own_out[:axes, :], own_out[axes:, :] = join_own(axes, own_ref, groups, weights)
    head, tail = join_group(axes, groups, weights)
    if last_stage is None:
        group_outs[0][:axes, :] = head
        group_outs[0][axes:, :] = tail
    else:
        put_sends(group_outs, last_stage, head, tail)


def weigh_last(axes, own, parts):
    width = own.shape[1] - LANES
    half = width + LANES // 2
    first = own[axes - 1 : axes, width : width + 1]
    last = own[axes - 1 : axes, half : half + 1]
    weights = []
    for part in parts:
        head = part[axes - 1 : axes, width : width + 1]
        tail = part[axes - 1 : axes, half : half + 1]
        weights.append(
            (
                jnp.maximum(same(head, first), same(tail, first)),
                jnp.maximum(same(head, last), same(tail, last)),
            )
        )
    return weights


def join_last(axes, own, parts, weights):
    head, tail = own[:axes, :], own[axes:, :]
    for part, (to_head, to_tail) in zip(parts, weights):
        value = part[...]
        head = head + to_head * value
        tail = tail + to_tail * value
    return head, tail


def find_frames(axes, columns, centre, live, flat_ref, offset_ref):
    found = list(columns)
    for index in range(axes):
        lead = found[index]
        length = jnp.sum(lead * lead, 1, keepdims=True)
        length = jnp.where(live, length, 1.0)
        for later in range(index + 1, axes):
            share = jnp.sum(lead * found[later], 1, keepdims=True) / length
            found[later] = found[later] - share * lead
        unit = lead / jnp.sqrt(length)
        put_strided(flat_ref, unit, index, axes)
        offset = jnp.sum(centre * unit, 1, keepdims=True)
        put_strided(offset_ref, jnp.broadcast_to(offset, (SLOTS, LANES)), index, axes)


def sweep_blocks(axes, points_ref, nodes_ref, first, flat_ref, offset_ref):
    rows, width = points_ref.shape
    frames = get_flat(flat_ref, SLOTS * axes).astype(BF16)
    offset = offset_ref[:, :1]
    moment = jnp.zeros((SLOTS * axes, width), F32)
    columns = jnp.zeros((SLOTS * axes, LANES), F32)
    spread = dot_nt(frames, points_ref[:BLOCK, :])
    for start in range(0, rows, BLOCK):
        block = points_ref[start : start + BLOCK, :]
        slot_of = nodes_ref[:, start : start + BLOCK] - first
        terms = spread - offset
        if start + BLOCK < rows:
            spread = dot_nt(frames, points_ref[start + BLOCK : start + 2 * BLOCK, :])
        kept = [
            jnp.where(slot_of == slot, terms[slot * axes : (slot + 1) * axes], 0.0)
            for slot in range(SLOTS)
        ]
        lifted = jnp.concatenate(kept, 0).astype(BF16)
        moment = moment + dot_nn(lifted, block)
        columns = columns + fold_lanes(lifted.astype(F32))
    return moment, jnp.sum(columns, 1, keepdims=True)


def project_blocks(axes, points_ref, nodes_ref, first, flat_ref, offset_ref, out_ref):
    rows = points_ref.shape[0]
    frames = get_flat(flat_ref, SLOTS * axes).astype(BF16)
    offset = offset_ref[:, :1]
    for start in range(0, rows, BLOCK):
        block = points_ref[start : start + BLOCK, :]
        slot_of = nodes_ref[:, start : start + BLOCK] - first
        terms = dot_nt(block, frames).T - offset
        out_ref[:, start : start + BLOCK] = sum(
            jnp.where(slot_of == slot, terms[slot * axes : (slot + 1) * axes], 0.0)
            for slot in range(SLOTS)
        )


def emit_part(axes, moment, column_sums, centre, span, part_ref, note_ref):
    for slot in range(SLOTS):
        at = slice(slot * axes, (slot + 1) * axes)
        part_ref[at, :] = moment[at] - column_sums[at] * centre[slot : slot + 1, :]
    tail = pl.multiple_of(span * axes, axes)
    note_ref[:axes, :] = part_ref[:axes, :]
    note_ref[axes:, :] = part_ref[pl.ds(tail, axes), :]


def live_slots(span):
    return lax.broadcasted_iota(jnp.int32, (SLOTS, 1), 0) <= span


def second_sweep_kernel(axes, count, points_ref, nodes_ref, init_ref, part_ref, sums_ref, own_ref, *refs):
    groups = refs[:count]
    part_out, note_out, centre_ref, weight_ref, flat_ref, offset_ref, whole_ref = refs[count:]
    width = points_ref.shape[1]
    first, last = ends_of(nodes_ref)
    span = last - first
    weights = weigh_last(axes, own_ref, groups)
    store_weights(weight_ref, weights)
    head, tail = join_last(axes, own_ref, groups, weights)
    flat = SLOTS * axes
    put_rows(whole_ref, part_ref[...], 0, flat)
    put_rows(whole_ref, tail[:, :width], pl.multiple_of(span * axes, axes), flat)
    put_rows(whole_ref, head[:, :width], 0, flat)
    counted = width // LANES
    slots = lax.broadcasted_iota(jnp.int32, (SLOTS, 1), 0)
    sums = sums_ref[:, :width]
    counts = sums_ref[:, width:]
    for slot, tile in ((span, tail[:, width:]), (0, head[:, width:])):
        sums = jnp.where(slots == slot, sums_of(tile, width), sums)
        counts = jnp.where(slots == slot, tile[counted : counted + 1], counts)
    live = live_slots(span)
    centre = sums / jnp.where(live, counts[:, :1], 1.0)
    centre_ref[...] = centre
    start = init_ref[...].astype(BF16).astype(F32)
    columns = []
    for index in range(axes):
        spread = jnp.sum(sums * start[index : index + 1], 1, keepdims=True)
        columns.append(get_strided(whole_ref, index, axes) - spread * centre)
    find_frames(axes, columns, centre, live, flat_ref, offset_ref)
    moment, column_sums = sweep_blocks(axes, points_ref, nodes_ref, first, flat_ref, offset_ref)
    emit_part(axes, moment, column_sums, centre_ref[...], span, part_out, note_out)


def settle_frames(axes, nodes_ref, part_ref, centre_ref, own_ref, weight_ref, groups, flat_ref, offset_ref, whole_ref):
    first, last = ends_of(nodes_ref)
    span = last - first
    weights = load_weights(weight_ref, len(groups), 2)
    head, tail = join_last(axes, own_ref, groups, weights)
    flat = SLOTS * axes
    put_rows(whole_ref, part_ref[...], 0, flat)
    put_rows(whole_ref, tail, pl.multiple_of(span * axes, axes), flat)
    put_rows(whole_ref, head, 0, flat)
    columns = [get_strided(whole_ref, index, axes) for index in range(axes)]
    find_frames(axes, columns, centre_ref[...], live_slots(span), flat_ref, offset_ref)
    return first, span


def sweep_kernel(axes, count, points_ref, nodes_ref, part_ref, centre_ref, own_ref, weight_ref, *refs):
    groups = refs[:count]
    part_out, note_out, flat_ref, offset_ref, whole_ref = refs[count:]
    first, span = settle_frames(
        axes, nodes_ref, part_ref, centre_ref, own_ref, weight_ref, groups, flat_ref, offset_ref, whole_ref
    )
    moment, column_sums = sweep_blocks(axes, points_ref, nodes_ref, first, flat_ref, offset_ref)
    emit_part(axes, moment, column_sums, centre_ref[...], span, part_out, note_out)


def project_kernel(axes, count, points_ref, nodes_ref, part_ref, centre_ref, own_ref, weight_ref, *refs):
    groups = refs[:count]
    out_ref, flat_ref, offset_ref, whole_ref = refs[count:]
    first, _ = settle_frames(
        axes, nodes_ref, part_ref, centre_ref, own_ref, weight_ref, groups, flat_ref, offset_ref, whole_ref
    )
    project_blocks(axes, points_ref, nodes_ref, first, flat_ref, offset_ref, out_ref)


def radices(size):
    found = []
    factor = 4
    while size > 1:
        while size % factor == 0:
            found.append(factor)
            size //= factor
        factor = 2 if factor == 4 else factor + 1
    return found


def stages_of(mesh):
    stages = []
    stride = 1
    for name in ("col", "row"):
        for radix in radices(mesh.shape[name]):
            stages.append((stride, radix))
            stride *= radix
    return stages


def swap(values, stage, devices):
    stride, radix = stage
    received = []
    for shift, value in enumerate(values, 1):
        pairs = []
        for source in range(devices):
            place = source // stride % radix
            pairs.append((source, source + (partner(place, shift, radix) - place) * stride))
        received.append(lax.ppermute(value, ("row", "col"), pairs))
    return received


def shape(*dims):
    return jax.ShapeDtypeStruct(dims, F32)


def call(kernel, outs, scratch=(), limit=8, source=pltpu.VMEM):
    vmem = pl.BlockSpec(memory_space=pltpu.VMEM)

    def run(*args):
        return pl.pallas_call(
            kernel,
            out_shape=outs,
            in_specs=[pl.BlockSpec(memory_space=source)] * len(args),
            out_specs=jax.tree.map(lambda _: vmem, outs),
            scratch_shapes=scratch,
            compiler_params=pltpu.CompilerParams(vmem_limit_bytes=limit * MIB),
        )(*args)

    return run


def solution(mesh):
    stages = stages_of(mesh)
    devices = mesh.shape["row"] * mesh.shape["col"]

    def shards(points, node_of_row, init_axes):
        rows, width = points.shape
        axes = init_axes.shape[1]
        flat = SLOTS * axes
        wide = width + LANES
        tall = flat * width // LANES
        frame_scratch = [pltpu.VMEM((tall, LANES), F32), pltpu.VMEM((flat, LANES), F32)]
        part, sums, note, points, nodes, init = call(
            functools.partial(first_sweep_kernel, axes),
            (
                shape(flat, width),
                shape(SLOTS, wide),
                shape(2 * axes, wide),
                jax.ShapeDtypeStruct((rows, width), points.dtype),
                jax.ShapeDtypeStruct((1, rows), node_of_row.dtype),
                shape(axes, width),
            ),
            [pltpu.SemaphoreType.DMA((len(cuts_of(rows)) + 1,))],
            limit=32,
            source=pltpu.HBM,
        )(*[pltpu.with_memory_space_constraint(each, pltpu.HBM) for each in (points, node_of_row.reshape(1, rows), init_axes.T)])
        own = note
        sends = [note]
        kept = []
        for index, stage in enumerate(stages[:-1]):
            groups = [sends[0]] + swap(sends * (stage[1] - 1), stage, devices)
            count = len(groups)
            ending = stages[-1] if index == len(stages) - 2 else None
            outs = [shape(2 * axes, wide)] if ending is None else [shape(axes, wide)] * (ending[1] - 1)
            own, weight, *sends = call(
                functools.partial(first_join_kernel, axes, count, ending),
                (shape(2 * axes, wide), shape(8 * count, LANES), *outs),
            )(own, *groups)
            kept.append(weight)
        groups = swap(sends, stages[-1], devices)[::-1]
        count = len(groups)
        part, note, centre, weight = call(
            functools.partial(second_sweep_kernel, axes, count),
            (shape(flat, width), shape(2 * axes, width), shape(SLOTS, width), shape(8 * count, LANES)),
            frame_scratch + [pltpu.VMEM((tall, LANES), F32)],
            limit=32,
        )(points, nodes, init, part, sums, own, *groups)
        kept.append(weight)
        for repeat in range(1, ITERS):
            own = note
            sends = [note]
            for index, stage in enumerate(stages[:-1]):
                groups = [sends[0]] + swap(sends * (stage[1] - 1), stage, devices)
                ending = stages[-1] if index == len(stages) - 2 else None
                outs = [shape(2 * axes, width)] if ending is None else [shape(axes, width)] * (ending[1] - 1)
                own, *sends = call(
                    functools.partial(join_kernel, axes, len(groups), ending),
                    (shape(2 * axes, width), *outs),
                )(own, kept[index], *groups)
            groups = swap(sends, stages[-1], devices)[::-1]
            settle = frame_scratch + [pltpu.VMEM((tall, LANES), F32)]
            if repeat < ITERS - 1:
                part, note = call(
                    functools.partial(sweep_kernel, axes, len(groups)),
                    (shape(flat, width), shape(2 * axes, width)),
                    settle,
                    limit=32,
                )(points, nodes, part, centre, own, kept[-1], *groups)
        return call(
            functools.partial(project_kernel, axes, len(groups)), shape(axes, rows), settle, limit=32
        )(points, nodes, part, centre, own, kept[-1], *groups)

    in_specs = (P(("row", "col"), None), P(("row", "col")), P())
    out_specs = P(None, ("row", "col"))
    return jax.shard_map(shards, mesh=mesh, in_specs=in_specs, out_specs=out_specs, check_vma=False)
```
